32 devices in a mesh: dp: 4 (over z), bank: 4 (over y, x), head: 2 (over core).
Axes of the slice: x: 2, y: 2, z: 4, core: 2. Of those that a mesh axis runs over, the one named last changes fastest.
Arguments:
- feats: bfloat16 [2048, 2048], P('dp'), may hold values from -6 to 6
- w_first: bfloat16 [2048, 2048], P(None, ('bank', 'head')), may hold values from -0.125 to 0.125
- w_second: bfloat16 [2048, 256], P(('bank', 'head')), may hold values from -0.125 to 0.125
- fresh_keys: float32 [2048, 256], P('dp'), may hold values from -6 to 6
- bank: float32 [32768, 256], P(('bank', 'head'))
- block_lists: int32 [4, 32], P('dp'), may hold values from 0 to 63, as said below
- dest_rows: int32 [2048], P('dp'), may hold values from 0 to 32767, as said below
Outputs:
- loss: float32 [2048], P('dp')
- grad_first: float32 [2048, 2048], P('dp', ('bank', 'head'))
- grad_second: float32 [2048, 256], P(('bank', 'head'))
- new_bank: float32 [32768, 256], P(('bank', 'head'))
The draws below stay inside these ranges and needn't reach their ends.
Inputs may be any that keep to these rules, and one draw needn't show every extreme that they name: `block_lists`: each row names 32 different blocks. `dest_rows`: all entries differ; the 512 entries of query block g name exactly 64 rows in each range of rows o * 4096 to (o + 1) * 4096 - 1.
All inputs are finite; a program needn't handle non-finite values.
Results may differ from the reference program's by a relative error of at most 0.012.
Values sent between devices are 32-bit elements; how exact they have to be, the bound alone decides.
A program may use at most 128 MiB of HBM per device.

```python
import jax
import jax.numpy as jnp
from jax import lax

DIN = 2048
HID = 2048
E = 256
BLOCK = 512
NNEG = 32
BLK_DEV = 8
OWNERS = 8
GROUPS = 4
BANK_DEV = 4096
BANK = 32768
NBLK = 64
Q_TOTAL = 2048
PER_OWN = 64
N_DP = 4


def draw_bank(key, part):
    first, second, third = jax.random.split(key, 3)
    row_scale = jnp.exp(jax.random.uniform(second, (BANK, 1), jnp.float32, jnp.log(0.02), jnp.log(0.2)))
    col_scale = jnp.exp(jax.random.uniform(third, (1, E), jnp.float32, jnp.log(0.5), jnp.log(5.0)))
    base = jax.random.normal(first, (BANK, E), jnp.float32)
    return (base * row_scale * col_scale).astype(jnp.float32)


def draw_block_lists(key, part):
    first, second = jax.random.split(key, 2)
    owner_heat = jax.random.randint(first, (OWNERS,), 0, 4)
    block_heat = jnp.repeat(owner_heat, BLK_DEV)
    noise = jax.random.randint(second, (GROUPS, NBLK), 0, 1 << 20)
    score = (noise + block_heat[None, :] * (1 << 19)) * NBLK + jnp.arange(NBLK)[None, :]
    group_ids = jnp.arange(GROUPS)[:, None]
    block_ids = jnp.arange(NBLK)[None, :]
    forced_last = (group_ids == 0) & (block_ids == NBLK - 1)
    forced_first = (group_ids == GROUPS - 1) & (block_ids == 0)
    score = jnp.where(forced_last | forced_first, 2147483647, score)
    unused, picked = jax.lax.top_k(score, NNEG)
    return picked.astype(jnp.int32)


def draw_dest_rows(key, part):
    first, second = jax.random.split(key, 2)
    owner_keys = jax.random.split(first, OWNERS)
    taken = GROUPS * PER_OWN

    def owner_rows(owner_key):
        middle = 1 + jax.random.permutation(owner_key, BANK_DEV - 2)[:taken - 2]
        ends = jnp.array([0, BANK_DEV - 1], jnp.int32)
        return jnp.concatenate([ends, middle.astype(jnp.int32)])
    local_rows = jax.vmap(owner_rows)(owner_keys).reshape(OWNERS, GROUPS, PER_OWN)
    values = jnp.transpose(local_rows, (1, 0, 2)) + (jnp.arange(OWNERS, dtype=jnp.int32) * BANK_DEV)[None, :, None]
    values = values.reshape(GROUPS, BLOCK)
    group_keys = jax.random.split(second, GROUPS)
    places = jax.vmap(lambda group_key: jax.random.permutation(group_key, BLOCK))(group_keys)
    empty = jnp.zeros((GROUPS, BLOCK), jnp.int32)
    filled = jax.vmap(lambda target, where_to, source: target.at[where_to].set(source))(empty, places, values)
    return filled.reshape(GROUPS * BLOCK).astype(jnp.int32)


def strengthened(values, rng, source, target, shards_of, factor):
    def block_of(position):
        return (jnp.arange(values.shape[position]) // (values.shape[position] // shards_of)).reshape((-1,) + (1,) * (values.ndim - 1 - position))

    first = jax.random.permutation(rng, shards_of)[block_of(target)]
    other_side = (block_of(target) + shards_of // 2) % shards_of
    return jnp.where((block_of(source) == first) | (block_of(source) == other_side), factor * values, values)


def level_of(stream_key, dims, shards, low, top_value):
    def one(axis_at, blocks):
        draws = jax.random.uniform(jax.random.fold_in(jax.random.fold_in(stream_key, 6), axis_at), (blocks,), jnp.float32, low / len(shards), top_value / len(shards))
        return jnp.repeat(jnp.exp(draws), dims[axis_at] // blocks).reshape((-1,) + (1,) * (len(dims) - axis_at - 1))

    factor_of = one(*shards[0])
    for cut in shards[1:]:
        factor_of = factor_of * one(*cut)
    return factor_of


def scatter_about(rng, shape, spread, limit, pieces=(), kind=jnp.bfloat16):
    values = jax.random.normal(rng, shape, jnp.float32) * spread
    if len(pieces) > 0:
        values = level_of(rng, shape, pieces, -0.22, 0.18) * values
    return jnp.clip(values, min=-limit, max=limit).astype(kind)


def gaussian_with(stream_key, dims, scale, bound, cuts, heavy, kind=jnp.bfloat16):
    entries = scale * jax.random.normal(stream_key, dims, jnp.float32)
    if cuts:
        entries = entries * level_of(stream_key, dims, cuts, -0.22, 0.18)
    return jnp.clip(strengthened(entries, jax.random.fold_in(stream_key, 3), *heavy), -bound, bound).astype(kind)


def setup_inputs(seed: int = 0) -> dict:
    key_of = jax.random.split(jax.random.key(seed), 8)
    return {
        "feats": gaussian_with(key_of[0], (Q_TOTAL, DIN), 1.0, 6.0, ((0, 4),), (0, 1, 4, 2.0)),
        "w_first": scatter_about(key_of[1], (DIN, HID), DIN ** -0.5, 0.125, ((1, 8),)),
        "w_second": scatter_about(key_of[2], (HID, E), HID ** -0.5, 0.125, ((0, 8),)),
        "fresh_keys": scatter_about(key_of[3], (Q_TOTAL, E), 1.0, 6.0, ((0, 4),), jnp.float32),
        "bank": draw_bank(jax.random.fold_in(key_of[7], 71), 0),
        "block_lists": draw_block_lists(jax.random.fold_in(key_of[7], 71), 0),
        "dest_rows": draw_dest_rows(jax.random.fold_in(key_of[7], 71), 0),
    }


sharpness_divisor = 0.2
epsilon = 1e-06

def unit_rows(values):
    norms = jnp.sqrt(lax.optimization_barrier(jnp.sum(values * values, axis=1, keepdims=True)) + epsilon)
    return (values / norms, norms)

def reference(feats, w_first, w_second, fresh_keys, bank, block_lists, dest_rows):
    hidden = jnp.maximum(jnp.dot(feats, w_first, preferred_element_type=jnp.float32), 0.0).astype(jnp.bfloat16)
    embed = jnp.dot(hidden, w_second, preferred_element_type=jnp.float32)
    anchor_matrix, norms = unit_rows(embed)
    unit_length_bank, unused = unit_rows(fresh_keys)
    matching_similarity = lax.optimization_barrier(jnp.sum(anchor_matrix * unit_length_bank, axis=1)) / sharpness_divisor
    blocks = bank.reshape(NBLK, BLOCK, E)

    def one_block(inputs):
        anchor_subset, pos_block, listed = inputs
        bank_entries = blocks[listed.astype(jnp.int32)].reshape(NNEG * BLOCK, E)
        similarity_matrix = lax.dot_general(anchor_subset, bank_entries, (((1,), (1,)), ((), ())), precision=lax.Precision.HIGHEST, preferred_element_type=jnp.float32) / sharpness_divisor
        best = jnp.maximum(lax.optimization_barrier(jnp.max(similarity_matrix, axis=1)), pos_block)
        weights = jnp.exp(similarity_matrix - best[:, None])
        positive_weight = jnp.exp(pos_block - best)
        partition_total = lax.optimization_barrier(jnp.sum(weights, axis=1)) + positive_weight
        probability_mixed_bank = jnp.dot(weights / partition_total[:, None], bank_entries, precision=lax.Precision.HIGHEST, preferred_element_type=jnp.float32)
        return (best + jnp.log(partition_total) - pos_block, probability_mixed_bank, positive_weight / partition_total)
    loss, probability_mixed_bank, matching_probability = lax.map(one_block, (anchor_matrix.reshape(N_DP, BLOCK, E), matching_similarity.reshape(N_DP, BLOCK), block_lists))
    loss = loss.reshape(Q_TOTAL)
    probability_mixed_bank = probability_mixed_bank.reshape(Q_TOTAL, E)
    matching_probability = matching_probability.reshape(Q_TOTAL)
    anchor_derivative = (probability_mixed_bank + (matching_probability - 1.0)[:, None] * unit_length_bank) / sharpness_divisor
    inner = lax.optimization_barrier(jnp.sum(anchor_matrix * anchor_derivative, axis=1, keepdims=True))
    grad_z = ((anchor_derivative - anchor_matrix * inner) / norms).astype(jnp.bfloat16)
    grad_second = lax.dot_general(hidden, grad_z, (((0,), (0,)), ((), ())), preferred_element_type=jnp.float32)
    grad_hidden = lax.dot_general(grad_z, w_second, (((1,), (1,)), ((), ())), preferred_element_type=jnp.float32)
    grad_pre = jnp.where(hidden > 0, grad_hidden, 0.0).astype(jnp.bfloat16)
    grad_first = lax.dot_general(feats, grad_pre, (((0,), (0,)), ((), ())), preferred_element_type=jnp.float32)
    new_bank = bank.at[dest_rows.astype(jnp.int32)].set(unit_length_bank)
    return (loss, grad_first, grad_second, new_bank)
```

```python
import functools
import math

import jax
import jax.numpy as jnp
from jax import lax
from jax.experimental import pallas as pl
from jax.experimental.pallas import tpu as pltpu
from jax.sharding import PartitionSpec as P

BLOCK = 512
EPS = 1e-6
SCALE = 5.0
LOG2E = 1.4426950408889634
LN2 = 0.6931471805599453
LOWEST = -1e30
MESH = pl.DeviceIdType.MESH
F32 = jnp.float32
BF16 = jnp.bfloat16


def nt(a, b, **kw):
    return lax.dot_general(a, b, (((1,), (1,)), ((), ())), preferred_element_type=F32, **kw)


def tn(a, b):
    return lax.dot_general(a, b, (((0,), (0,)), ((), ())), preferred_element_type=F32)


def body(
    D, N, H,
    feats, w1, w2, fresh, bank, bias, dest,
    loss_out, gf_out, gs_out, keys_out, kd_out,
    hid, zp, zr, zs, zfull, kcat, qcat, sbuf, acc, ml, ar, mr, st, gz, gfull, lt, lr,
    gfs, gfr, gsp, gsr, gst, gsf, ks, kr, kd, kdr,
    s_z, r_z, s_q, r_q, s_a, r_a, s_m, r_m, s_g, r_g, s_l, r_l,
    s_f, r_f, s_s, r_s, s_t, r_t, s_k, r_k, s_d, r_d,
):
    d = lax.axis_index("dp")
    bk = lax.axis_index("bank")
    hd = lax.axis_index("head")
    me = bk * H + hd
    rows = zp.shape[0]
    R = rows // N
    nblk = kcat.shape[0]

    def plane(k):
        p = lax.rem(me + k, N)
        return p, {"bank": lax.div(p, H), "head": lax.rem(p, H)}

    def line(j):
        p = lax.rem(d + j, D)
        return p, {"dp": p}

    def chunk(p, size):
        return pl.ds(pl.multiple_of(p * size, size), size)

    def send(src, dst, ss, rs, dev):
        c = pltpu.make_async_remote_copy(
            src_ref=src, dst_ref=dst, send_sem=ss, recv_sem=rs,
            device_id=dev, device_id_type=MESH)
        c.start()
        return c

    barrier = pltpu.get_barrier_semaphore()
    for k in range(1, N):
        pl.semaphore_signal(barrier, inc=1, device_id=plane(k)[1], device_id_type=MESH)
    for j in range(1, D):
        pl.semaphore_signal(barrier, inc=1, device_id=line(j)[1], device_id_type=MESH)

    h = jnp.maximum(jnp.dot(feats[...], w1[...], preferred_element_type=F32), 0.0).astype(BF16)
    hid[...] = h
    zp[...] = jnp.dot(h, w2[...], preferred_element_type=F32)
    pl.semaphore_wait(barrier, N - 1 + D - 1)

    pending = []
    z_copies = []
    for k in range(1, N):
        p, dev = plane(k)
        z_copies.append(send(zp.at[chunk(p, R)], zr.at[k], s_z.at[k], r_z.at[k], dev))

    f = fresh[...]
    unit = f / jnp.sqrt(jnp.sum(f * f, axis=1, keepdims=True) + EPS)
    local = dest[...] - (me * bank.shape[0]).astype(F32)
    inside = (local >= 0.0) & (local < float(bank.shape[0]))
    one = jnp.where(inside, 1.0, 0.0)
    upper = lax.broadcasted_iota(jnp.int32, (rows, rows), 0) <= lax.broadcasted_iota(
        jnp.int32, (rows, rows), 1)
    place = jnp.dot(one.astype(BF16), jnp.where(upper, 1.0, 0.0).astype(BF16),
                    preferred_element_type=F32) * one
    want = lax.broadcasted_iota(jnp.int32, (128, rows), 0).astype(F32) + 1.0
    pick = jnp.where(want == jnp.broadcast_to(place[0:1, :], (128, rows)), 1.0, 0.0)
    ks[...] = jnp.dot(pick[0:R], unit, precision=lax.Precision.HIGHEST, preferred_element_type=F32)
    kd[...] = nt(jnp.where(inside, local, 0.0), pick, precision=lax.Precision.HIGHEST)
    for j in range(1, D):
        dev = line(j)[1]
        pending.append(send(ks, kr.at[j], s_k.at[j], r_k.at[j], dev))
        pending.append(send(kd, kdr.at[j], s_d.at[j], r_d.at[j], dev))
    kr[0] = ks[...]
    kdr[0] = kd[...]

    def split(b, carry):
        x = bank[pl.ds(pl.multiple_of(b * BLOCK, BLOCK), BLOCK), :]
        hi = x.astype(BF16)
        lo = (x - hi.astype(F32)).astype(BF16)
        kcat[b, :, 0:256] = hi
        kcat[b, :, 256:512] = lo
        kcat[b, :, 512:768] = hi
        return carry

    lax.fori_loop(0, nblk, split, 0)

    total_z = zp[chunk(me, R), :]
    for k in range(1, N):
        z_copies[k - 1].wait_recv()
        total_z = total_z + zr[k]
    zs[...] = total_z
    zfull[chunk(me, R), :] = total_z
    q_copies = []
    for k in range(1, N):
        dev = plane(k)[1]
        q_copies.append(send(zs, zfull.at[chunk(me, R)], s_q.at[k], r_q.at[k], dev))
    for c in q_copies:
        c.wait_recv()
    z = zfull[...]
    q = z / jnp.sqrt(jnp.sum(z * z, axis=1, keepdims=True) + EPS) * (SCALE * LOG2E)
    qh = q.astype(BF16)
    qcat[:, 0:256] = qh
    qcat[:, 256:512] = qh
    qcat[:, 512:768] = (q - qh.astype(F32)).astype(BF16)

    def scores(b, best):
        s = nt(qcat[...], kcat[b]) + bias[b]
        sbuf[b] = s
        for t in range(BLOCK // 128):
            best = jnp.maximum(best, s[:, t * 128:(t + 1) * 128])
        return best

    best = lax.fori_loop(0, nblk, scores, jnp.full((rows, 128), LOWEST, F32))
    best = jnp.max(best, axis=1, keepdims=True)
    acc[...] = jnp.zeros_like(acc)

    def mix(b, total):
        w = jnp.exp2(sbuf[b] - best)
        for t in range(BLOCK // 128):
            total = total + w[:, t * 128:(t + 1) * 128]
        both = jnp.dot(w.astype(BF16), kcat[b, :, 0:512], preferred_element_type=F32)
        acc[...] += both[:, 0:256] + both[:, 256:512]
        return total

    total = lax.fori_loop(0, nblk, mix, jnp.zeros((rows, 128), F32))
    total = jnp.sum(total, axis=1, keepdims=True)
    lane = lax.broadcasted_iota(jnp.int32, (rows, 128), 1)
    stat = jnp.where(lane == 0, best, total).T
    for c in range(rows // 128):
        ml[c] = stat[0:8, c * 128:(c + 1) * 128]

    a_copies = []
    per = 128 // R
    for k in range(1, N):
        p, dev = plane(k)
        a_copies.append(send(ml.at[lax.div(p, per)], mr.at[k], s_m.at[k], r_m.at[k], dev))
        a_copies.append(send(acc.at[chunk(p, R)], ar.at[k], s_a.at[k], r_a.at[k], dev))
    mr[0] = ml[lax.div(me, per)]
    for c in a_copies:
        c.wait_recv()
    tiles = mr[...].reshape(N * 8, 128)
    st[...] = jnp.concatenate([tiles, jnp.zeros((128 - N * 8, 128), F32)], axis=0).T
    stats = st[chunk(lax.rem(me, per), R), :]

    zc = zfull[chunk(me, R), :]
    norm = jnp.sqrt(jnp.sum(zc * zc, axis=1, keepdims=True) + EPS)
    qc = zc / norm
    fc = fresh[chunk(me, R), :]
    uc = fc / jnp.sqrt(jnp.sum(fc * fc, axis=1, keepdims=True) + EPS)
    pos = jnp.sum(qc * uc, axis=1, keepdims=True) * (SCALE * LOG2E)
    top = pos
    for k in range(N):
        top = jnp.maximum(top, stats[:, k * 8:k * 8 + 1])
    pw = jnp.exp2(pos - top)
    den = pw
    mixed = jnp.zeros((R, acc.shape[1]), F32)
    for k in range(N):
        wk = jnp.exp2(stats[:, k * 8:k * 8 + 1] - top)
        den = den + wk * stats[:, k * 8 + 1:k * 8 + 2]
        mixed = mixed + wk * (acc[chunk(me, R), :] if k == 0 else ar[k])
    losses = (top - pos) * LN2 + jnp.log(den)
    gq = (mixed / den + (pw / den - 1.0) * uc) * SCALE
    inner = jnp.sum(qc * gq, axis=1, keepdims=True)
    g = ((gq - qc * inner) / norm).astype(BF16).astype(F32)
    gz[...] = g
    gfull[chunk(me, R), :] = g
    wide = jnp.concatenate(
        [jnp.broadcast_to(losses, (R, 128)), jnp.zeros((128 - R, 128), F32)], axis=0)
    lt[...] = wide.T[0:8, :]
    lr[me] = lt[...]
    g_copies = []
    for k in range(1, N):
        dev = plane(k)[1]
        g_copies.append(send(gz, gfull.at[chunk(me, R)], s_g.at[k], r_g.at[k], dev))
        pending.append(send(lt, lr.at[me], s_l.at[k], r_l.at[k], dev))
    for c in g_copies:
        c.wait_recv()

    gb = gfull[...].astype(BF16)
    gsp[...] = tn(hid[...], gb)
    S = gsp.shape[0] // D
    s_copies = []
    for j in range(1, D):
        p, dev = line(j)
        s_copies.append(send(gsp.at[chunk(p, S)], gsr.at[j], s_s.at[j], r_s.at[j], dev))
    gp = nt(gb, w2[...])
    gp = jnp.where(hid[...] > 0, gp, 0.0).astype(BF16)
    F = gf_out.shape[0]
    f_copies = []
    if F % 128:
        for t in range(feats.shape[1] // 256):
            gfs[t * 256:(t + 1) * 256, :] = tn(feats[:, t * 256:(t + 1) * 256], gp)
    for j in [*range(1, D), 0]:
        p, dev = line(j)
        if F % 128 == 0:
            gfs[chunk(p, F), :] = tn(feats[:, chunk(p, F)], gp)
        if j:
            f_copies.append(send(gfs.at[chunk(p, F)], gfr.at[j], s_f.at[j], r_f.at[j], dev))

    total_s = gsp[chunk(d, S), :]
    for j in range(1, D):
        s_copies[j - 1].wait_recv()
        total_s = total_s + gsr[j]
    gst[...] = total_s
    gsf[chunk(d, S), :] = total_s
    t_copies = []
    for j in range(1, D):
        dev = line(j)[1]
        t_copies.append(send(gst, gsf.at[chunk(d, S)], s_t.at[j], r_t.at[j], dev))

    for c in pending:
        c.wait_recv()
    keys_out[...] = kr[...].reshape(keys_out.shape)
    kd_out[...] = kdr[...]
    loss_out[...] = lr[...]
    for c in t_copies:
        c.wait_recv()
    gs_out[...] = gsf[...]
    gf_out[...] = gfs[chunk(d, F), :]
    for j in range(1, D):
        f_copies[j - 1].wait_recv()
        gf_out[...] += gfr[j]
    for c in z_copies + q_copies + a_copies + g_copies + s_copies + t_copies + f_copies + pending:
        c.wait_send()


def shards(D, N, H, feats, w_first, w_second, fresh_keys, bank, block_lists, dest_rows):
    owner = lax.axis_index(("bank", "head"))
    rows, din = feats.shape
    hcols = w_first.shape[1]
    E = w_second.shape[1]
    nblk = bank.shape[0] // BLOCK
    R = rows // N
    F = din // D
    S = hcols // D
    mine = owner * nblk + jnp.arange(nblk, dtype=jnp.int32)
    owned = jnp.any(block_lists[0][None, :] == mine[:, None], axis=1)
    bias = jnp.where(owned, 0.0, LOWEST).astype(F32)
    dest = jnp.broadcast_to(dest_rows.astype(F32)[None, :], (8, rows))
    V = pl.BlockSpec(memory_space=pltpu.VMEM)
    sds = jax.ShapeDtypeStruct
    vm = pltpu.VMEM
    scratch = [
        vm((rows, hcols), BF16), vm((rows, E), F32), vm((N, R, E), F32), vm((R, E), F32),
        vm((rows, E), F32), vm((nblk, BLOCK, 3 * E), BF16), vm((rows, 3 * E), BF16),
        vm((nblk, rows, BLOCK), F32), vm((rows, E), F32), vm((rows // 128, 8, 128), F32),
        vm((N, R, E), F32), vm((N, 8, 128), F32), vm((128, 128), F32), vm((R, E), F32),
        vm((rows, E), F32), vm((8, 128), F32), vm((N, 8, 128), F32),
        vm((din, hcols), F32), vm((D, F, hcols), F32), vm((hcols, E), F32), vm((D, S, E), F32),
        vm((S, E), F32), vm((hcols, E), F32), vm((R, E), F32), vm((D, R, E), F32),
        vm((8, 128), F32), vm((D, 8, 128), F32),
    ]
    dma = pltpu.SemaphoreType.DMA
    sems = [dma((N,))] * 12 + [dma((D,))] * 10
    loss, grad_first, grad_second, keys, kdest = pl.pallas_call(
        functools.partial(body, D, N, H),
        out_shape=(
            sds((N, 8, 128), F32), sds((F, hcols), F32), sds((hcols, E), F32),
            sds((D * R, E), F32), sds((D, 8, 128), F32),
        ),
        in_specs=[V, V, V, V, V, pl.BlockSpec(memory_space=pltpu.SMEM), V],
        out_specs=(V,) * 5,
        scratch_shapes=scratch + sems,
        compiler_params=pltpu.CompilerParams(
            collective_id=0, has_side_effects=True, vmem_limit_bytes=56 * 1024 * 1024),
    )(feats, w_first, w_second, fresh_keys, bank, bias, dest)
    index = jnp.round(kdest[:, 0, :R]).astype(jnp.int32).reshape(D * R)
    new_bank = bank.at[index].set(keys, unique_indices=True, mode="promise_in_bounds")
    return (loss[:, 0, :R].reshape(rows), grad_first, grad_second, new_bank)


def solution(mesh):
    D = mesh.shape["dp"]
    H = mesh.shape["head"]
    N = mesh.shape["bank"] * H
    return jax.shard_map(
        functools.partial(shards, D, N, H),
        mesh=mesh,
        in_specs=(
            P("dp", None),
            P(None, ("bank", "head")),
            P(("bank", "head"), None),
            P("dp", None),
            P(("bank", "head"), None),
            P("dp", None),
            P("dp"),
        ),
        out_specs=(
            P("dp"),
            P("dp", ("bank", "head")),
            P(("bank", "head"), None),
            P(("bank", "head"), None),
        ),
        check_vma=False,
    )
```

```python
import functools
import math

import jax
import jax.numpy as jnp
from jax import lax
from jax.experimental import pallas as pl
from jax.experimental.pallas import tpu as pltpu
from jax.sharding import PartitionSpec as P

BLOCK = 512
EPS = 1e-6
SCALE = 5.0
LOG2E = 1.4426950408889634
LN2 = 0.6931471805599453
LOWEST = -1e30
MESH = pl.DeviceIdType.MESH
F32 = jnp.float32
BF16 = jnp.bfloat16


def nt(a, b, **kw):
    return lax.dot_general(a, b, (((1,), (1,)), ((), ())), preferred_element_type=F32, **kw)


def tn(a, b):
    return lax.dot_general(a, b, (((0,), (0,)), ((), ())), preferred_element_type=F32)


def body(
    D, N, H,
    feats, w1, w2, fresh, bank, lists, dest,
    loss_out, gf_out, gs_out, keys_out, kd_out,
    hid, zp, zr, zs, zfull, kcat, qcat, sbuf, acc, ml, ar, mr, st, gz, gfull, lt, lr,
    gfs, gfr, gfl, gsp, gsr, gst, gsf, ks, kr, kd, kdr,
    s_z, r_z, s_q, r_q, s_a, r_a, s_m, r_m, s_g, r_g, s_l, r_l,
    s_f, r_f, s_s, r_s, s_t, r_t, s_k, r_k, s_d, r_d, s_fl, r_fl, bvm, s_b,
):
    d = lax.axis_index("dp")
    bk = lax.axis_index("bank")
    hd = lax.axis_index("head")
    me = bk * H + hd
    rows = zp.shape[0]
    R = rows // N
    nblk = kcat.shape[0]

    def plane(k):
        p = lax.rem(me + k, N)
        return p, {"bank": lax.div(p, H), "head": lax.rem(p, H)}

    def line(j):
        p = lax.rem(d + j, D)
        return p, {"dp": p}

    def chunk(p, size):
        return pl.ds(pl.multiple_of(p * size, size), size)

    def send(src, dst, ss, rs, dev):
        c = pltpu.make_async_remote_copy(
            src_ref=src, dst_ref=dst, send_sem=ss, recv_sem=rs,
            device_id=dev, device_id_type=MESH)
        c.start()
        return c

    def load(b):
        at = pl.ds(pl.multiple_of(b * BLOCK, BLOCK), BLOCK)
        return pltpu.make_async_copy(bank.at[at], bvm.at[at], s_b.at[b])

    for b in range(nblk):
        load(b).start()
    barrier = pltpu.get_barrier_semaphore()
    for k in range(1, N):
        pl.semaphore_signal(barrier, inc=1, device_id=plane(k)[1], device_id_type=MESH)
    for j in range(1, D):
        pl.semaphore_signal(barrier, inc=1, device_id=line(j)[1], device_id_type=MESH)

    h = jnp.maximum(jnp.dot(feats[...], w1[...], preferred_element_type=F32), 0.0).astype(BF16)
    hid[...] = h
    zp[...] = jnp.dot(h, w2[...], preferred_element_type=F32)
    pl.semaphore_wait(barrier, N - 1 + D - 1)

    pending = []
    z_copies = []
    for k in range(1, N):
        p, dev = plane(k)
        z_copies.append(send(zp.at[chunk(p, R)], zr.at[k], s_z.at[k], r_z.at[k], dev))

    f = fresh[...]
    unit = f / jnp.sqrt(jnp.sum(f * f, axis=1, keepdims=True) + EPS)
    local = jnp.broadcast_to(dest[...].astype(F32), (8, rows)) - (me * bank.shape[0]).astype(F32)
    inside = (local >= 0.0) & (local < float(bank.shape[0]))
    one = jnp.where(inside, 1.0, 0.0)
    upper = lax.broadcasted_iota(jnp.int32, (rows, rows), 0) <= lax.broadcasted_iota(
        jnp.int32, (rows, rows), 1)
    place = jnp.dot(one.astype(BF16), jnp.where(upper, 1.0, 0.0).astype(BF16),
                    preferred_element_type=F32) * one
    want = lax.broadcasted_iota(jnp.int32, (128, rows), 0).astype(F32) + 1.0
    pick = jnp.where(want == jnp.broadcast_to(place[0:1, :], (128, rows)), 1.0, 0.0)
    ks[...] = jnp.dot(pick[0:R], unit, precision=lax.Precision.HIGHEST, preferred_element_type=F32)
    kd[...] = nt(jnp.where(inside, local, 0.0), pick, precision=lax.Precision.HIGHEST)
    for j in range(1, D):
        dev = line(j)[1]
        pending.append(send(ks, kr.at[j], s_k.at[j], r_k.at[j], dev))
        pending.append(send(kd, kdr.at[j], s_d.at[j], r_d.at[j], dev))
    kr[0] = ks[...]
    kdr[0] = kd[...]

    def split(b, carry):
        load(b).wait()
        x = bvm[pl.ds(pl.multiple_of(b * BLOCK, BLOCK), BLOCK), :]
        hi = x.astype(BF16)
        lo = (x - hi.astype(F32)).astype(BF16)
        kcat[b, :, 0:256] = hi
        kcat[b, :, 256:512] = lo
        kcat[b, :, 512:768] = hi
        return carry

    lax.fori_loop(0, nblk, split, 0)

    total_z = zp[chunk(me, R), :]
    for k in range(1, N):
        z_copies[k - 1].wait_recv()
        total_z = total_z + zr[k]
    zs[...] = total_z
    zfull[chunk(me, R), :] = total_z
    q_copies = []
    for k in range(1, N):
        dev = plane(k)[1]
        q_copies.append(send(zs, zfull.at[chunk(me, R)], s_q.at[k], r_q.at[k], dev))
    for c in q_copies:
        c.wait_recv()
    z = zfull[...]
    q = z / jnp.sqrt(jnp.sum(z * z, axis=1, keepdims=True) + EPS) * (SCALE * LOG2E)
    qh = q.astype(BF16)
    qcat[:, 0:256] = qh
    qcat[:, 256:512] = qh
    qcat[:, 512:768] = (q - qh.astype(F32)).astype(BF16)

    def scores(b, best):
        hit = jnp.max(jnp.where(lists[...] == me * nblk + b, 0.0, LOWEST), axis=1, keepdims=True)
        s = nt(qcat[...], kcat[b]) + hit
        sbuf[b] = s
        for t in range(BLOCK // 128):
            best = jnp.maximum(best, s[:, t * 128:(t + 1) * 128])
        return best

    best = lax.fori_loop(0, nblk, scores, jnp.full((rows, 128), LOWEST, F32))
    best = jnp.max(best, axis=1, keepdims=True)
    acc[...] = jnp.zeros_like(acc)

    def mix(b, total):
        w = jnp.exp2(sbuf[b] - best)
        for t in range(BLOCK // 128):
            total = total + w[:, t * 128:(t + 1) * 128]
        both = jnp.dot(w.astype(BF16), kcat[b, :, 0:512], preferred_element_type=F32)
        acc[...] += both[:, 0:256] + both[:, 256:512]
        return total

    total = lax.fori_loop(0, nblk, mix, jnp.zeros((rows, 128), F32))
    total = jnp.sum(total, axis=1, keepdims=True)
    lane = lax.broadcasted_iota(jnp.int32, (rows, 128), 1)
    stat = jnp.where(lane == 0, best, total).T
    for c in range(rows // 128):
        ml[c] = stat[0:8, c * 128:(c + 1) * 128]

    a_copies = []
    per = 128 // R
    for k in range(1, N):
        p, dev = plane(k)
        a_copies.append(send(ml.at[lax.div(p, per)], mr.at[k], s_m.at[k], r_m.at[k], dev))
        a_copies.append(send(acc.at[chunk(p, R)], ar.at[k], s_a.at[k], r_a.at[k], dev))
    mr[0] = ml[lax.div(me, per)]
    for c in a_copies:
        c.wait_recv()
    tiles = mr[...].reshape(N * 8, 128)
    st[...] = jnp.concatenate([tiles, jnp.zeros((128 - N * 8, 128), F32)], axis=0).T
    stats = st[chunk(lax.rem(me, per), R), :]

    zc = zfull[chunk(me, R), :]
    norm = jnp.sqrt(jnp.sum(zc * zc, axis=1, keepdims=True) + EPS)
    qc = zc / norm
    fc = fresh[chunk(me, R), :]
    uc = fc / jnp.sqrt(jnp.sum(fc * fc, axis=1, keepdims=True) + EPS)
    pos = jnp.sum(qc * uc, axis=1, keepdims=True) * (SCALE * LOG2E)
    top = pos
    for k in range(N):
        top = jnp.maximum(top, stats[:, k * 8:k * 8 + 1])
    pw = jnp.exp2(pos - top)
    den = pw
    mixed = jnp.zeros((R, acc.shape[1]), F32)
    for k in range(N):
        wk = jnp.exp2(stats[:, k * 8:k * 8 + 1] - top)
        den = den + wk * stats[:, k * 8 + 1:k * 8 + 2]
        mixed = mixed + wk * (acc[chunk(me, R), :] if k == 0 else ar[k])
    losses = (top - pos) * LN2 + jnp.log(den)
    gq = (mixed / den + (pw / den - 1.0) * uc) * SCALE
    inner = jnp.sum(qc * gq, axis=1, keepdims=True)
    g = ((gq - qc * inner) / norm).astype(BF16).astype(F32)
    gz[...] = g
    gfull[chunk(me, R), :] = g
    wide = jnp.concatenate(
        [jnp.broadcast_to(losses, (R, 128)), jnp.zeros((128 - R, 128), F32)], axis=0)
    lt[...] = wide.T[0:8, :]
    lr[me] = lt[...]
    g_copies = []
    for k in range(1, N):
        dev = plane(k)[1]
        g_copies.append(send(gz, gfull.at[chunk(me, R)], s_g.at[k], r_g.at[k], dev))
        pending.append(send(lt, lr.at[me], s_l.at[k], r_l.at[k], dev))
    for c in g_copies:
        c.wait_recv()

    gb = gfull[...].astype(BF16)
    gsp[...] = tn(hid[...], gb)
    S = gsp.shape[0] // D
    s_copies = []
    for j in range(1, D):
        p, dev = line(j)
        s_copies.append(send(gsp.at[chunk(p, S)], gsr.at[j], s_s.at[j], r_s.at[j], dev))
    gp = nt(gb, w2[...])
    gp = jnp.where(hid[...] > 0, gp, 0.0).astype(BF16)
    F = gf_out.shape[0]
    if F % 128:
        for t in range(feats.shape[1] // 256):
            gfs[t * 256:(t + 1) * 256, :] = tn(feats[:, t * 256:(t + 1) * 256], gp)

    def hop(p, nxt, got, ss, rs):
        return pltpu.make_async_remote_copy(
            src_ref=gfs.at[chunk(p, F)], dst_ref=got.at[p], send_sem=ss.at[p],
            recv_sem=rs.at[p], device_id={"dp": nxt}, device_id_type=MESH)

    def step(p, first, nxt, got, ss, rs):
        if F % 128 == 0:
            gfs[chunk(p, F), :] = tn(feats[:, chunk(p, F)], gp)
        move = hop(p, nxt, got, ss, rs)

        @pl.when(jnp.logical_not(first))
        def _():
            move.wait_recv()
            gfs[chunk(p, F), :] += got[p]

        move.start()

    up = lax.min(d + 1, D - 1)
    down = lax.max(d - 1, 0)

    def both_ways(t, act):
        @pl.when(d <= t)
        def _():
            act(D - 1 - t + d, d == 0, up, gfr, s_f, r_f)

        @pl.when(d >= D - 1 - t)
        def _():
            act(t - (D - 1 - d), d == D - 1, down, gfl, s_fl, r_fl)

    t_copies = []
    for t in range(D - 1):
        both_ways(t, step)
        if t == 0:
            total_s = gsp[chunk(d, S), :]
            for j in range(1, D):
                s_copies[j - 1].wait_recv()
                total_s = total_s + gsr[j]
            gst[...] = total_s
            gsf[chunk(d, S), :] = total_s
            for j in range(1, D):
                dev = line(j)[1]
                t_copies.append(send(gst, gsf.at[chunk(d, S)], s_t.at[j], r_t.at[j], dev))
    if F % 128 == 0:
        gf_out[...] = tn(feats[:, chunk(d, F)], gp)
    else:
        gf_out[...] = gfs[chunk(d, F), :]

    for c in pending:
        c.wait_recv()
    keys_out[...] = kr[...].reshape(keys_out.shape)
    kd_out[...] = kdr[...]
    loss_out[...] = lr[...]
    for c in t_copies:
        c.wait_recv()
    gs_out[...] = gsf[...]

    @pl.when(d > 0)
    def _():
        hop(d, up, gfr, s_f, r_f).wait_recv()
        gf_out[...] += gfr[d]

    @pl.when(d < D - 1)
    def _():
        hop(d, down, gfl, s_fl, r_fl).wait_recv()
        gf_out[...] += gfl[d]

    for t in range(D - 1):
        both_ways(t, lambda p, first, nxt, got, ss, rs: hop(p, nxt, got, ss, rs).wait_send())
    for c in z_copies + q_copies + a_copies + g_copies + s_copies + t_copies + pending:
        c.wait_send()


def place_rows(D, R, bank, keys, where, out, sem):
    copy = pltpu.make_async_copy(bank, out, sem)
    copy.start()
    copy.wait()

    def group(i, carry):
        j = lax.div(i, R // 8)
        first = lax.rem(i, R // 8) * 8
        for t in range(8):
            row = (where[j, 0, first + t] + 0.5).astype(jnp.int32)
            out[pl.ds(row, 1), :] = keys[pl.ds(i * 8 + t, 1), :]
        return carry

    lax.fori_loop(0, D * R // 8, group, 0)


def shards(D, N, H, feats, w_first, w_second, fresh_keys, bank, block_lists, dest_rows):
    rows, din = feats.shape
    hcols = w_first.shape[1]
    E = w_second.shape[1]
    nblk = bank.shape[0] // BLOCK
    R = rows // N
    F = din // D
    S = hcols // D
    V = pl.BlockSpec(memory_space=pltpu.VMEM)
    ANY = pl.BlockSpec(memory_space=pl.ANY)
    sds = jax.ShapeDtypeStruct
    vm = pltpu.VMEM
    scratch = [
        vm((rows, hcols), BF16), vm((rows, E), F32), vm((N, R, E), F32), vm((R, E), F32),
        vm((rows, E), F32), vm((nblk, BLOCK, 3 * E), BF16), vm((rows, 3 * E), BF16),
        vm((nblk, rows, BLOCK), F32), vm((rows, E), F32), vm((rows // 128, 8, 128), F32),
        vm((N, R, E), F32), vm((N, 8, 128), F32), vm((128, 128), F32), vm((R, E), F32),
        vm((rows, E), F32), vm((8, 128), F32), vm((N, 8, 128), F32),
        vm((din, hcols), F32), vm((D, F, hcols), F32), vm((D, F, hcols), F32), vm((hcols, E), F32), vm((D, S, E), F32),
        vm((S, E), F32), vm((hcols, E), F32), vm((R, E), F32), vm((D, R, E), F32),
        vm((8, 128), F32), vm((D, 8, 128), F32),
    ]
    dma = pltpu.SemaphoreType.DMA
    sems = [dma((N,))] * 12 + [dma((D,))] * 12 + [vm(bank.shape, F32), dma((nblk,))]
    loss, grad_first, grad_second, keys, kdest = pl.pallas_call(
        functools.partial(body, D, N, H),
        out_shape=(
            sds((N, 8, 128), F32), sds((F, hcols), F32), sds((hcols, E), F32),
            sds((D * R, E), F32), sds((D, 8, 128), F32),
        ),
        in_specs=[V, V, V, V, ANY, V, V],
        out_specs=(V,) * 5,
        scratch_shapes=scratch + sems,
        compiler_params=pltpu.CompilerParams(
            collective_id=0, has_side_effects=True, vmem_limit_bytes=56 * 1024 * 1024),
    )(feats, w_first, w_second, fresh_keys, bank, block_lists, dest_rows.reshape(1, rows))
    new_bank = pl.pallas_call(
        functools.partial(place_rows, D, R),
        out_shape=sds(bank.shape, F32),
        in_specs=[ANY, V, pl.BlockSpec(memory_space=pltpu.SMEM)],
        out_specs=V,
        scratch_shapes=[dma],
        compiler_params=pltpu.CompilerParams(vmem_limit_bytes=16 * 1024 * 1024),
    )(bank, keys, kdest)
    return (loss[:, 0, :R].reshape(rows), grad_first, grad_second, new_bank)


def solution(mesh):
    D = mesh.shape["dp"]
    H = mesh.shape["head"]
    N = mesh.shape["bank"] * H
    return jax.shard_map(
        functools.partial(shards, D, N, H),
        mesh=mesh,
        in_specs=(
            P("dp", None),
            P(None, ("bank", "head")),
            P(("bank", "head"), None),
            P("dp", None),
            P(("bank", "head"), None),
            P("dp", None),
            P("dp"),
        ),
        out_specs=(
            P("dp"),
            P("dp", ("bank", "head")),
            P(("bank", "head"), None),
            P(("bank", "head"), None),
        ),
        check_vma=False,
    )
```

```python
import functools
import math

import jax
import jax.numpy as jnp
from jax import lax
from jax.experimental import pallas as pl
from jax.experimental.pallas import tpu as pltpu
from jax.sharding import PartitionSpec as P

BLOCK = 512
EPS = 1e-6
SCALE = 5.0
LOG2E = 1.4426950408889634
LN2 = 0.6931471805599453
LOWEST = -1e30
MESH = pl.DeviceIdType.MESH
F32 = jnp.float32
BF16 = jnp.bfloat16


def nt(a, b, **kw):
    return lax.dot_general(a, b, (((1,), (1,)), ((), ())), preferred_element_type=F32, **kw)


def tn(a, b):
    return lax.dot_general(a, b, (((0,), (0,)), ((), ())), preferred_element_type=F32)


def body(
    D, N, H,
    feats, w1, w2, fresh, bank, lists, dest,
    loss_out, gf_out, gs_out, bank_out,
    hid, zp, zr, zs, zfull, kcat, qcat, sbuf, acc, ml, ar, mr, st, gz, gfull, lt, lr,
    gfs, gfr, gfl, gsp, gsr, gst, gsf, ks, kr, kd, kdr,
    s_z, r_z, s_q, r_q, s_a, r_a, s_m, r_m, s_g, r_g, s_l, r_l,
    s_f, r_f, s_s, r_s, s_t, r_t, s_k, r_k, s_d, r_d, s_fl, r_fl, bvm, s_b, s_o, k3,
):
    d = lax.axis_index("dp")
    bk = lax.axis_index("bank")
    hd = lax.axis_index("head")
    me = bk * H + hd
    rows = zp.shape[0]
    R = rows // N
    nblk = kcat.shape[0]

    def plane(k):
        p = lax.rem(me + k, N)
        return p, {"bank": lax.div(p, H), "head": lax.rem(p, H)}

    def line(j):
        p = lax.rem(d + j, D)
        return p, {"dp": p}

    def chunk(p, size):
        return pl.ds(pl.multiple_of(p * size, size), size)

    def send(src, dst, ss, rs, dev):
        c = pltpu.make_async_remote_copy(
            src_ref=src, dst_ref=dst, send_sem=ss, recv_sem=rs,
            device_id=dev, device_id_type=MESH)
        c.start()
        return c

    def load(b):
        at = pl.ds(pl.multiple_of(b * BLOCK, BLOCK), BLOCK)
        return pltpu.make_async_copy(bank.at[at], bvm.at[at], s_b.at[b])

    for b in range(nblk):
        load(b).start()
    C = N // H
    sibling = {"head": 1 - hd}

    def gather_rows(mine, full, ss, rs):
        at = full.at[chunk(me, R)]
        away = []
        for i in range(1, C):
            dev = {"bank": lax.rem(bk + i, C)}
            away.append(send(mine, at, ss.at[i], rs.at[i], dev))
        near = [send(mine, at, ss.at[C], rs.at[C], sibling)]
        for i in range(1, C):
            away[i - 1].wait_recv()
            came = full.at[chunk(lax.rem(bk + C - i, C) * H + hd, R)]
            near.append(send(came, came, ss.at[C + i], rs.at[C + i], sibling))
        for c in near:
            c.wait_recv()
        return away + near

    barrier = pltpu.get_barrier_semaphore()
    for k in range(1, N):
        pl.semaphore_signal(barrier, inc=1, device_id=plane(k)[1], device_id_type=MESH)
    for j in range(1, D):
        pl.semaphore_signal(barrier, inc=1, device_id=line(j)[1], device_id_type=MESH)

    h = jnp.maximum(jnp.dot(feats[...], w1[...], preferred_element_type=F32), 0.0).astype(BF16)
    hid[...] = h
    zp[...] = jnp.dot(h, w2[...], preferred_element_type=F32)
    pl.semaphore_wait(barrier, N - 1 + D - 1)

    pending = []
    z_copies = []
    for k in range(1, N):
        p, dev = plane(k)
        z_copies.append(send(zp.at[chunk(p, R)], zr.at[k], s_z.at[k], r_z.at[k], dev))

    f = fresh[...]
    unit = f / jnp.sqrt(jnp.sum(f * f, axis=1, keepdims=True) + EPS)
    local = jnp.broadcast_to(dest[...].astype(F32), (8, rows)) - (me * bank.shape[0]).astype(F32)
    inside = (local >= 0.0) & (local < float(bank.shape[0]))
    one = jnp.where(inside, 1.0, 0.0)
    upper = lax.broadcasted_iota(jnp.int32, (rows, rows), 0) <= lax.broadcasted_iota(
        jnp.int32, (rows, rows), 1)
    place = jnp.dot(one.astype(BF16), jnp.where(upper, 1.0, 0.0).astype(BF16),
                    preferred_element_type=F32) * one
    want = lax.broadcasted_iota(jnp.int32, (128, rows), 0).astype(F32) + 1.0
    pick = jnp.where(want == jnp.broadcast_to(place[0:1, :], (128, rows)), 1.0, 0.0)
    ks[...] = jnp.dot(pick[0:R], unit, precision=lax.Precision.HIGHEST, preferred_element_type=F32)
    spots = nt(jnp.where(inside, local, 0.0), pick, precision=lax.Precision.HIGHEST)
    kd[...] = jnp.floor(spots + 0.5)
    for j in range(1, D):
        dev = line(j)[1]
        pending.append(send(ks, kr.at[j], s_k.at[j], r_k.at[j], dev))
        pending.append(send(kd, kdr.at[j], s_d.at[j], r_d.at[j], dev))
    kr[0] = ks[...]
    kdr[0] = kd[...]

    def split(b, carry):
        load(b).wait()
        x = bvm[pl.ds(pl.multiple_of(b * BLOCK, BLOCK), BLOCK), :]
        hi = x.astype(BF16)
        lo = (x - hi.astype(F32)).astype(BF16)
        kcat[b, :, 0:256] = hi
        kcat[b, :, 256:512] = lo
        kcat[b, :, 512:768] = hi
        return carry

    lax.fori_loop(0, nblk, split, 0)

    total_z = zp[chunk(me, R), :]
    for k in range(1, N):
        z_copies[k - 1].wait_recv()
        total_z = total_z + zr[k]
    zs[...] = total_z
    zfull[chunk(me, R), :] = total_z
    q_copies = gather_rows(zs, zfull, s_q, r_q)
    z = zfull[...]
    q = z / jnp.sqrt(jnp.sum(z * z, axis=1, keepdims=True) + EPS) * (SCALE * LOG2E)
    qh = q.astype(BF16)
    qcat[:, 0:256] = qh
    qcat[:, 256:512] = qh
    qcat[:, 512:768] = (q - qh.astype(F32)).astype(BF16)

    def scores(b, best):
        hit = jnp.max(jnp.where(lists[...] == me * nblk + b, 0.0, LOWEST), axis=1, keepdims=True)
        s = nt(qcat[...], kcat[b]) + hit
        sbuf[b] = s
        for t in range(BLOCK // 128):
            best = jnp.maximum(best, s[:, t * 128:(t + 1) * 128])
        return best

    best = lax.fori_loop(0, nblk, scores, jnp.full((rows, 128), LOWEST, F32))
    best = jnp.max(best, axis=1, keepdims=True)
    acc[...] = jnp.zeros_like(acc)

    def mix(b, total):
        w = jnp.exp2(sbuf[b] - best)
        for t in range(BLOCK // 128):
            total = total + w[:, t * 128:(t + 1) * 128]
        both = jnp.dot(w.astype(BF16), kcat[b, :, 0:512], preferred_element_type=F32)
        acc[...] += both[:, 0:256] + both[:, 256:512]
        return total

    total = lax.fori_loop(0, nblk, mix, jnp.zeros((rows, 128), F32))
    total = jnp.sum(total, axis=1, keepdims=True)
    lane = lax.broadcasted_iota(jnp.int32, (rows, 128), 1)
    stat = jnp.where(lane == 0, best, total).T
    for c in range(rows // 128):
        ml[c] = stat[0:8, c * 128:(c + 1) * 128]

    a_copies = []
    per = 128 // R
    for k in range(1, N):
        p, dev = plane(k)
        a_copies.append(send(ml.at[lax.div(p, per)], mr.at[k], s_m.at[k], r_m.at[k], dev))
        a_copies.append(send(acc.at[chunk(p, R)], ar.at[k], s_a.at[k], r_a.at[k], dev))
    mr[0] = ml[lax.div(me, per)]
    for c in a_copies:
        c.wait_recv()
    tiles = mr[...].reshape(N * 8, 128)
    st[...] = jnp.concatenate([tiles, jnp.zeros((128 - N * 8, 128), F32)], axis=0).T
    stats = st[chunk(lax.rem(me, per), R), :]

    zc = zfull[chunk(me, R), :]
    norm = jnp.sqrt(jnp.sum(zc * zc, axis=1, keepdims=True) + EPS)
    qc = zc / norm
    fc = fresh[chunk(me, R), :]
    uc = fc / jnp.sqrt(jnp.sum(fc * fc, axis=1, keepdims=True) + EPS)
    pos = jnp.sum(qc * uc, axis=1, keepdims=True) * (SCALE * LOG2E)
    top = pos
    for k in range(N):
        top = jnp.maximum(top, stats[:, k * 8:k * 8 + 1])
    pw = jnp.exp2(pos - top)
    den = pw
    mixed = jnp.zeros((R, acc.shape[1]), F32)
    for k in range(N):
        wk = jnp.exp2(stats[:, k * 8:k * 8 + 1] - top)
        den = den + wk * stats[:, k * 8 + 1:k * 8 + 2]
        mixed = mixed + wk * (acc[chunk(me, R), :] if k == 0 else ar[k])
    losses = (top - pos) * LN2 + jnp.log(den)
    gq = (mixed / den + (pw / den - 1.0) * uc) * SCALE
    inner = jnp.sum(qc * gq, axis=1, keepdims=True)
    g = ((gq - qc * inner) / norm).astype(BF16).astype(F32)
    gz[...] = g
    gfull[chunk(me, R), :] = g
    wide = jnp.concatenate(
        [jnp.broadcast_to(losses, (R, 128)), jnp.zeros((128 - R, 128), F32)], axis=0)
    lt[...] = wide.T[0:8, :]
    lr[me] = lt[...]
    for k in range(1, N):
        pending.append(send(lt, lr.at[me], s_l.at[k], r_l.at[k], plane(k)[1]))
    g_copies = gather_rows(gz, gfull, s_g, r_g)

    gb = gfull[...].astype(BF16)
    gsp[...] = tn(hid[...], gb)
    S = gsp.shape[0] // D
    s_copies = []
    for j in range(1, D):
        p, dev = line(j)
        s_copies.append(send(gsp.at[chunk(p, S)], gsr.at[j], s_s.at[j], r_s.at[j], dev))
    gp = nt(gb, w2[...])
    gp = jnp.where(hid[...] > 0, gp, 0.0).astype(BF16)
    F = gf_out.shape[0]
    if F % 128:
        for t in range(feats.shape[1] // 256):
            gfs[t * 256:(t + 1) * 256, :] = tn(feats[:, t * 256:(t + 1) * 256], gp)

    def hop(p, nxt, got, ss, rs):
        return pltpu.make_async_remote_copy(
            src_ref=gfs.at[chunk(p, F)], dst_ref=got.at[p], send_sem=ss.at[p],
            recv_sem=rs.at[p], device_id={"dp": nxt}, device_id_type=MESH)

    def step(p, first, nxt, got, ss, rs):
        if F % 128 == 0:
            gfs[chunk(p, F), :] = tn(feats[:, chunk(p, F)], gp)
        move = hop(p, nxt, got, ss, rs)

        @pl.when(jnp.logical_not(first))
        def _():
            move.wait_recv()
            gfs[chunk(p, F), :] += got[p]

        move.start()

    up = lax.min(d + 1, D - 1)
    down = lax.max(d - 1, 0)

    def both_ways(t, act):
        @pl.when(d <= t)
        def _():
            act(D - 1 - t + d, d == 0, up, gfr, s_f, r_f)

        @pl.when(d >= D - 1 - t)
        def _():
            act(t - (D - 1 - d), d == D - 1, down, gfl, s_fl, r_fl)

    t_copies = []
    for t in range(D - 1):
        both_ways(t, step)
        if t == 0:
            total_s = gsp[chunk(d, S), :]
            for j in range(1, D):
                s_copies[j - 1].wait_recv()
                total_s = total_s + gsr[j]
            gst[...] = total_s
            gsf[chunk(d, S), :] = total_s
            for j in range(1, D):
                dev = line(j)[1]
                t_copies.append(send(gst, gsf.at[chunk(d, S)], s_t.at[j], r_t.at[j], dev))
    if F % 128 == 0:
        gf_out[...] = tn(feats[:, chunk(d, F)], gp)
    else:
        gf_out[...] = gfs[chunk(d, F), :]

    for c in pending:
        c.wait_recv()
    spot = jnp.concatenate([kdr[j][0:1, 0:R] for j in range(D)], axis=1)
    k = kr[...].reshape(D * R, kr.shape[2])
    k_hi = k.astype(BF16)
    k = k - k_hi.astype(F32)
    k_mid = k.astype(BF16)
    k3[:, 0:256] = k_hi
    k3[:, 256:512] = k_mid
    k3[:, 512:768] = (k - k_mid.astype(F32)).astype(BF16)

    def store(b):
        at = pl.ds(pl.multiple_of(b * BLOCK, BLOCK), BLOCK)
        return pltpu.make_async_copy(bvm.at[at], bank_out.at[at], s_o.at[b])

    def place_block(b, carry):
        row = (lax.broadcasted_iota(jnp.int32, (BLOCK, D * R), 0) + b * BLOCK).astype(F32)
        one_hot = jnp.where(row == spot, 1.0, 0.0)
        new = jnp.dot(one_hot.astype(BF16), k3[...], preferred_element_type=F32)
        new = new[:, 0:256] + new[:, 256:512] + new[:, 512:768]
        hit = jnp.max(one_hot, axis=1, keepdims=True) > 0.0
        at = pl.ds(pl.multiple_of(b * BLOCK, BLOCK), BLOCK)
        bvm[at, :] = jnp.where(hit, new, bvm[at, :])
        store(b).start()
        return carry

    lax.fori_loop(0, nblk, place_block, 0)
    loss_out[...] = lr[...]
    for c in t_copies:
        c.wait_recv()
    gs_out[...] = gsf[...]

    @pl.when(d > 0)
    def _():
        hop(d, up, gfr, s_f, r_f).wait_recv()
        gf_out[...] += gfr[d]

    @pl.when(d < D - 1)
    def _():
        hop(d, down, gfl, s_fl, r_fl).wait_recv()
        gf_out[...] += gfl[d]

    for b in range(nblk):
        store(b).wait()
    for t in range(D - 1):
        both_ways(t, lambda p, first, nxt, got, ss, rs: hop(p, nxt, got, ss, rs).wait_send())
    for c in z_copies + q_copies + a_copies + g_copies + s_copies + t_copies + pending:
        c.wait_send()


def shards(D, N, H, feats, w_first, w_second, fresh_keys, bank, block_lists, dest_rows):
    rows, din = feats.shape
    hcols = w_first.shape[1]
    E = w_second.shape[1]
    nblk = bank.shape[0] // BLOCK
    R = rows // N
    F = din // D
    S = hcols // D
    V = pl.BlockSpec(memory_space=pltpu.VMEM)
    ANY = pl.BlockSpec(memory_space=pl.ANY)
    sds = jax.ShapeDtypeStruct
    vm = pltpu.VMEM
    scratch = [
        vm((rows, hcols), BF16), vm((rows, E), F32), vm((N, R, E), F32), vm((R, E), F32),
        vm((rows, E), F32), vm((nblk, BLOCK, 3 * E), BF16), vm((rows, 3 * E), BF16),
        vm((nblk, rows, BLOCK), F32), vm((rows, E), F32), vm((rows // 128, 8, 128), F32),
        vm((N, R, E), F32), vm((N, 8, 128), F32), vm((128, 128), F32), vm((R, E), F32),
        vm((rows, E), F32), vm((8, 128), F32), vm((N, 8, 128), F32),
        vm((din, hcols), F32), vm((D, F, hcols), F32), vm((D, F, hcols), F32), vm((hcols, E), F32), vm((D, S, E), F32),
        vm((S, E), F32), vm((hcols, E), F32), vm((R, E), F32), vm((D, R, E), F32),
        vm((8, 128), F32), vm((D, 8, 128), F32),
    ]
    dma = pltpu.SemaphoreType.DMA
    sems = [dma((N,))] * 12 + [dma((D,))] * 12 + [vm(bank.shape, F32), dma((nblk,)), dma((nblk,)), vm((D * R, 3 * E), BF16)]
    loss, grad_first, grad_second, new_bank = pl.pallas_call(
        functools.partial(body, D, N, H),
        out_shape=(
            sds((N, 8, 128), F32), sds((F, hcols), F32), sds((hcols, E), F32),
            sds(bank.shape, F32),
        ),
        in_specs=[V, V, V, V, ANY, V, V],
        out_specs=(V, V, V, ANY),
        scratch_shapes=scratch + sems,
        compiler_params=pltpu.CompilerParams(
            collective_id=0, has_side_effects=True, vmem_limit_bytes=56 * 1024 * 1024),
    )(feats, w_first, w_second, fresh_keys, bank, block_lists, dest_rows.reshape(1, rows))
    return (loss[:, 0, :R].reshape(rows), grad_first, grad_second, new_bank)


def solution(mesh):
    D = mesh.shape["dp"]
    H = mesh.shape["head"]
    N = mesh.shape["bank"] * H
    return jax.shard_map(
        functools.partial(shards, D, N, H),
        mesh=mesh,
        in_specs=(
            P("dp", None),
            P(None, ("bank", "head")),
            P(("bank", "head"), None),
            P("dp", None),
            P(("bank", "head"), None),
            P("dp", None),
            P("dp"),
        ),
        out_specs=(
            P("dp"),
            P("dp", ("bank", "head")),
            P(("bank", "head"), None),
            P(("bank", "head"), None),
        ),
        check_vma=False,
    )
```

```python
import functools
import math

import jax
import jax.numpy as jnp
from jax import lax
from jax.experimental import pallas as pl
from jax.experimental.pallas import tpu as pltpu
from jax.sharding import PartitionSpec as P

BLOCK = 512
EPS = 1e-6
SCALE = 5.0
LOG2E = 1.4426950408889634
LN2 = 0.6931471805599453
LOWEST = -1e30
MESH = pl.DeviceIdType.MESH
F32 = jnp.float32
BF16 = jnp.bfloat16


def nt(a, b, **kw):
    return lax.dot_general(a, b, (((1,), (1,)), ((), ())), preferred_element_type=F32, **kw)


def tn(a, b):
    return lax.dot_general(a, b, (((0,), (0,)), ((), ())), preferred_element_type=F32)


def body(
    D, N, H,
    feats, w1, w2, fresh, bank, lists, dest,
    loss_out, gf_out, gs_out, bank_out,
    hid, zp, zr, zs, zfull, kcat, qcat, sbuf, acc, ml, ar, mr, st, gz, gfull, lt, lr,
    gfs, gfr, gfl, gsp, gsr, gst, gsf, ks, kr, kd, kdr,
    s_z, r_z, s_q, r_q, s_a, r_a, s_m, r_m, s_g, r_g, s_l, r_l,
    s_f, r_f, s_s, r_s, s_t, r_t, s_k, r_k, s_d, r_d, s_fl, r_fl, bvm, s_b, s_o, k3, zh,
):
    d = lax.axis_index("dp")
    bk = lax.axis_index("bank")
    hd = lax.axis_index("head")
    me = bk * H + hd
    rows = zp.shape[0]
    R = rows // N
    nblk = kcat.shape[0]

    def plane(k):
        p = lax.rem(me + k, N)
        return p, {"bank": lax.div(p, H), "head": lax.rem(p, H)}

    def line(j):
        p = lax.rem(d + j, D)
        return p, {"dp": p}

    def chunk(p, size):
        return pl.ds(pl.multiple_of(p * size, size), size)

    def send(src, dst, ss, rs, dev):
        c = pltpu.make_async_remote_copy(
            src_ref=src, dst_ref=dst, send_sem=ss, recv_sem=rs,
            device_id=dev, device_id_type=MESH)
        c.start()
        return c

    def load(b):
        at = pl.ds(pl.multiple_of(b * BLOCK, BLOCK), BLOCK)
        return pltpu.make_async_copy(bank.at[at], bvm.at[at], s_b.at[b])

    for b in range(nblk):
        load(b).start()
    C = N // H
    sibling = {"head": 1 - hd}

    def gather_rows(mine, full, ss, rs):
        at = full.at[chunk(me, R)]
        away = []
        for i in range(1, C):
            dev = {"bank": lax.rem(bk + i, C)}
            away.append(send(mine, at, ss.at[i], rs.at[i], dev))
        near = [send(mine, at, ss.at[C], rs.at[C], sibling)]
        for i in range(1, C):
            away[i - 1].wait_recv()
            came = full.at[chunk(lax.rem(bk + C - i, C) * H + hd, R)]
            near.append(send(came, came, ss.at[C + i], rs.at[C + i], sibling))
        for c in near:
            c.wait_recv()
        return away + near

    barrier = pltpu.get_barrier_semaphore()
    for k in range(1, N):
        pl.semaphore_signal(barrier, inc=1, device_id=plane(k)[1], device_id_type=MESH)
    for j in range(1, D):
        pl.semaphore_signal(barrier, inc=1, device_id=line(j)[1], device_id_type=MESH)

    h = jnp.maximum(jnp.dot(feats[...], w1[...], preferred_element_type=F32), 0.0).astype(BF16)
    hid[...] = h
    zp[...] = jnp.dot(h, w2[...], preferred_element_type=F32)
    pl.semaphore_wait(barrier, N - 1 + D - 1)

    pending = []
    z_copies = []
    turns = [*range(1, C), 0]
    for i in turns:
        part = zp.at[chunk(lax.rem(bk + i, C) * H + 1 - hd, R)]
        z_copies.append(send(part, zr.at[i], s_z.at[i], r_z.at[i], sibling))
    z_away = []
    for i in turns:
        z_copies[turns.index(i)].wait_recv()
        c = lax.rem(bk + i, C)
        zh[i] = zp[chunk(c * H + hd, R), :] + zr[i]
        if i:
            z_away.append(send(zh.at[i], zr.at[C + i], s_z.at[C + i], r_z.at[C + i], {"bank": c}))

    f = fresh[...]
    unit = f / jnp.sqrt(jnp.sum(f * f, axis=1, keepdims=True) + EPS)
    local = jnp.broadcast_to(dest[...].astype(F32), (8, rows)) - (me * bank.shape[0]).astype(F32)
    inside = (local >= 0.0) & (local < float(bank.shape[0]))
    one = jnp.where(inside, 1.0, 0.0)
    upper = lax.broadcasted_iota(jnp.int32, (rows, rows), 0) <= lax.broadcasted_iota(
        jnp.int32, (rows, rows), 1)
    place = jnp.dot(one.astype(BF16), jnp.where(upper, 1.0, 0.0).astype(BF16),
                    preferred_element_type=F32) * one
    want = lax.broadcasted_iota(jnp.int32, (128, rows), 0).astype(F32) + 1.0
    pick = jnp.where(want == jnp.broadcast_to(place[0:1, :], (128, rows)), 1.0, 0.0)
    ks[...] = jnp.dot(pick[0:R], unit, precision=lax.Precision.HIGHEST, preferred_element_type=F32)
    spots = nt(jnp.where(inside, local, 0.0), pick, precision=lax.Precision.HIGHEST)
    kd[...] = jnp.floor(spots + 0.5)
    for j in range(1, D):
        dev = line(j)[1]
        pending.append(send(ks, kr.at[j], s_k.at[j], r_k.at[j], dev))
        pending.append(send(kd, kdr.at[j], s_d.at[j], r_d.at[j], dev))
    kr[0] = ks[...]
    kdr[0] = kd[...]

    def split(b, carry):
        load(b).wait()
        x = bvm[pl.ds(pl.multiple_of(b * BLOCK, BLOCK), BLOCK), :]
        hi = x.astype(BF16)
        lo = (x - hi.astype(F32)).astype(BF16)
        kcat[b, :, 0:256] = hi
        kcat[b, :, 256:512] = lo
        kcat[b, :, 512:768] = hi
        return carry

    lax.fori_loop(0, nblk, split, 0)

    total_z = zh[0]
    for i in range(1, C):
        z_away[i - 1].wait_recv()
        total_z = total_z + zr[C + i]
    zs[...] = total_z
    zfull[chunk(me, R), :] = total_z
    q_copies = gather_rows(zs, zfull, s_q, r_q)
    z = zfull[...]
    q = z / jnp.sqrt(jnp.sum(z * z, axis=1, keepdims=True) + EPS) * (SCALE * LOG2E)
    qh = q.astype(BF16)
    qcat[:, 0:256] = qh
    qcat[:, 256:512] = qh
    qcat[:, 512:768] = (q - qh.astype(F32)).astype(BF16)

    def scores(b, best):
        hit = jnp.max(jnp.where(lists[...] == me * nblk + b, 0.0, LOWEST), axis=1, keepdims=True)
        s = nt(qcat[...], kcat[b]) + hit
        sbuf[b] = s
        for t in range(BLOCK // 128):
            best = jnp.maximum(best, s[:, t * 128:(t + 1) * 128])
        return best

    best = lax.fori_loop(0, nblk, scores, jnp.full((rows, 128), LOWEST, F32))
    best = jnp.max(best, axis=1, keepdims=True)
    acc[...] = jnp.zeros_like(acc)

    def mix(b, total):
        w = jnp.exp2(sbuf[b] - best)
        for t in range(BLOCK // 128):
            total = total + w[:, t * 128:(t + 1) * 128]
        both = jnp.dot(w.astype(BF16), kcat[b, :, 0:512], preferred_element_type=F32)
        acc[...] += both[:, 0:256] + both[:, 256:512]
        return total

    total = lax.fori_loop(0, nblk, mix, jnp.zeros((rows, 128), F32))
    total = jnp.sum(total, axis=1, keepdims=True)
    lane = lax.broadcasted_iota(jnp.int32, (rows, 128), 1)
    stat = jnp.where(lane == 0, best, total).T
    for c in range(rows // 128):
        ml[c] = stat[0:8, c * 128:(c + 1) * 128]

    a_copies = []
    per = 128 // R
    for k in range(1, N):
        p, dev = plane(k)
        a_copies.append(send(ml.at[lax.div(p, per)], mr.at[k], s_m.at[k], r_m.at[k], dev))
        a_copies.append(send(acc.at[chunk(p, R)], ar.at[k], s_a.at[k], r_a.at[k], dev))
    mr[0] = ml[lax.div(me, per)]
    for c in a_copies:
        c.wait_recv()
    tiles = mr[...].reshape(N * 8, 128)
    st[...] = jnp.concatenate([tiles, jnp.zeros((128 - N * 8, 128), F32)], axis=0).T
    stats = st[chunk(lax.rem(me, per), R), :]

    zc = zfull[chunk(me, R), :]
    norm = jnp.sqrt(jnp.sum(zc * zc, axis=1, keepdims=True) + EPS)
    qc = zc / norm
    fc = fresh[chunk(me, R), :]
    uc = fc / jnp.sqrt(jnp.sum(fc * fc, axis=1, keepdims=True) + EPS)
    pos = jnp.sum(qc * uc, axis=1, keepdims=True) * (SCALE * LOG2E)
    top = pos
    for k in range(N):
        top = jnp.maximum(top, stats[:, k * 8:k * 8 + 1])
    pw = jnp.exp2(pos - top)
    den = pw
    mixed = jnp.zeros((R, acc.shape[1]), F32)
    for k in range(N):
        wk = jnp.exp2(stats[:, k * 8:k * 8 + 1] - top)
        den = den + wk * stats[:, k * 8 + 1:k * 8 + 2]
        mixed = mixed + wk * (acc[chunk(me, R), :] if k == 0 else ar[k])
    losses = (top - pos) * LN2 + jnp.log(den)
    gq = (mixed / den + (pw / den - 1.0) * uc) * SCALE
    inner = jnp.sum(qc * gq, axis=1, keepdims=True)
    g = ((gq - qc * inner) / norm).astype(BF16).astype(F32)
    gz[...] = g
    gfull[chunk(me, R), :] = g
    wide = jnp.concatenate(
        [jnp.broadcast_to(losses, (R, 128)), jnp.zeros((128 - R, 128), F32)], axis=0)
    lt[...] = wide.T[0:8, :]
    lr[me] = lt[...]
    for k in range(1, N):
        pending.append(send(lt, lr.at[me], s_l.at[k], r_l.at[k], plane(k)[1]))
    g_copies = gather_rows(gz, gfull, s_g, r_g)

    gb = gfull[...].astype(BF16)
    gsp[...] = tn(hid[...], gb)
    S = gsp.shape[0] // D
    s_copies = []
    for j in range(1, D):
        p, dev = line(j)
        s_copies.append(send(gsp.at[chunk(p, S)], gsr.at[j], s_s.at[j], r_s.at[j], dev))
    gp = nt(gb, w2[...])
    gp = jnp.where(hid[...] > 0, gp, 0.0).astype(BF16)
    F = gf_out.shape[0]
    if F % 128:
        for t in range(feats.shape[1] // 256):
            gfs[t * 256:(t + 1) * 256, :] = tn(feats[:, t * 256:(t + 1) * 256], gp)

    def hop(p, nxt, got, ss, rs):
        return pltpu.make_async_remote_copy(
            src_ref=gfs.at[chunk(p, F)], dst_ref=got.at[p], send_sem=ss.at[p],
            recv_sem=rs.at[p], device_id={"dp": nxt}, device_id_type=MESH)

    def step(p, first, nxt, got, ss, rs):
        if F % 128 == 0:
            gfs[chunk(p, F), :] = tn(feats[:, chunk(p, F)], gp)
        move = hop(p, nxt, got, ss, rs)

        @pl.when(jnp.logical_not(first))
        def _():
            move.wait_recv()
            gfs[chunk(p, F), :] += got[p]

        move.start()

    up = lax.min(d + 1, D - 1)
    down = lax.max(d - 1, 0)

    def both_ways(t, act):
        @pl.when(d <= t)
        def _():
            act(D - 1 - t + d, d == 0, up, gfr, s_f, r_f)

        @pl.when(d >= D - 1 - t)
        def _():
            act(t - (D - 1 - d), d == D - 1, down, gfl, s_fl, r_fl)

    t_copies = []
    for t in range(D - 1):
        both_ways(t, step)
        if t == 0:
            total_s = gsp[chunk(d, S), :]
            for j in range(1, D):
                s_copies[j - 1].wait_recv()
                total_s = total_s + gsr[j]
            gst[...] = total_s
            gsf[chunk(d, S), :] = total_s
            for j in range(1, D):
                dev = line(j)[1]
                t_copies.append(send(gst, gsf.at[chunk(d, S)], s_t.at[j], r_t.at[j], dev))
    if F % 128 == 0:
        gf_out[...] = tn(feats[:, chunk(d, F)], gp)
    else:
        gf_out[...] = gfs[chunk(d, F), :]

    for c in pending:
        c.wait_recv()
    spot = jnp.concatenate([kdr[j][0:1, 0:R] for j in range(D)], axis=1)
    k = kr[...].reshape(D * R, kr.shape[2])
    k_hi = k.astype(BF16)
    k = k - k_hi.astype(F32)
    k_mid = k.astype(BF16)
    k3[:, 0:256] = k_hi
    k3[:, 256:512] = k_mid
    k3[:, 512:768] = (k - k_mid.astype(F32)).astype(BF16)

    def store(b):
        at = pl.ds(pl.multiple_of(b * BLOCK, BLOCK), BLOCK)
        return pltpu.make_async_copy(bvm.at[at], bank_out.at[at], s_o.at[b])

    def place_block(b, carry):
        row = (lax.broadcasted_iota(jnp.int32, (BLOCK, D * R), 0) + b * BLOCK).astype(F32)
        one_hot = jnp.where(row == spot, 1.0, 0.0)
        new = jnp.dot(one_hot.astype(BF16), k3[...], preferred_element_type=F32)
        new = new[:, 0:256] + new[:, 256:512] + new[:, 512:768]
        hit = jnp.max(one_hot, axis=1, keepdims=True) > 0.0
        at = pl.ds(pl.multiple_of(b * BLOCK, BLOCK), BLOCK)
        bvm[at, :] = jnp.where(hit, new, bvm[at, :])
        store(b).start()
        return carry

    lax.fori_loop(0, nblk, place_block, 0)
    loss_out[...] = lr[...]
    for c in t_copies:
        c.wait_recv()
    gs_out[...] = gsf[...]

    @pl.when(d > 0)
    def _():
        hop(d, up, gfr, s_f, r_f).wait_recv()
        gf_out[...] += gfr[d]

    @pl.when(d < D - 1)
    def _():
        hop(d, down, gfl, s_fl, r_fl).wait_recv()
        gf_out[...] += gfl[d]

    for b in range(nblk):
        store(b).wait()
    for t in range(D - 1):
        both_ways(t, lambda p, first, nxt, got, ss, rs: hop(p, nxt, got, ss, rs).wait_send())
    for c in z_copies + z_away + q_copies + a_copies + g_copies + s_copies + t_copies + pending:
        c.wait_send()


def hand_on(gf, gs, bank, gf_out, gs_out, bank_out, sems):
    size = bank.shape[0] // 8
    copies = [
        pltpu.make_async_copy(
            bank.at[i * size:(i + 1) * size], bank_out.at[i * size:(i + 1) * size], sems.at[i])
        for i in range(8)
    ]
    copies.append(pltpu.make_async_copy(gf, gf_out, sems.at[8]))
    copies.append(pltpu.make_async_copy(gs, gs_out, sems.at[9]))
    for c in copies:
        c.start()
    for c in copies:
        c.wait()


def shards(D, N, H, feats, w_first, w_second, fresh_keys, bank, block_lists, dest_rows):
    rows, din = feats.shape
    hcols = w_first.shape[1]
    E = w_second.shape[1]
    nblk = bank.shape[0] // BLOCK
    R = rows // N
    F = din // D
    S = hcols // D
    V = pl.BlockSpec(memory_space=pltpu.VMEM)
    ANY = pl.BlockSpec(memory_space=pl.ANY)
    sds = jax.ShapeDtypeStruct
    vm = pltpu.VMEM
    scratch = [
        vm((rows, hcols), BF16), vm((rows, E), F32), vm((N, R, E), F32), vm((R, E), F32),
        vm((rows, E), F32), vm((nblk, BLOCK, 3 * E), BF16), vm((rows, 3 * E), BF16),
        vm((nblk, rows, BLOCK), F32), vm((rows, E), F32), vm((rows // 128, 8, 128), F32),
        vm((N, R, E), F32), vm((N, 8, 128), F32), vm((128, 128), F32), vm((R, E), F32),
        vm((rows, E), F32), vm((8, 128), F32), vm((N, 8, 128), F32),
        vm((din, hcols), F32), vm((D, F, hcols), F32), vm((D, F, hcols), F32), vm((hcols, E), F32), vm((D, S, E), F32),
        vm((S, E), F32), vm((hcols, E), F32), vm((R, E), F32), vm((D, R, E), F32),
        vm((8, 128), F32), vm((D, 8, 128), F32),
    ]
    dma = pltpu.SemaphoreType.DMA
    sems = [dma((N,))] * 12 + [dma((D,))] * 12 + [vm(bank.shape, F32), dma((nblk,)), dma((nblk,)), vm((D * R, 3 * E), BF16), vm((N // H, R, E), F32)]
    loss, grad_first, grad_second, new_bank = pl.pallas_call(
        functools.partial(body, D, N, H),
        out_shape=(
            sds((N, 8, 128), F32), sds((F, hcols), F32), sds((hcols, E), F32),
            sds(bank.shape, F32),
        ),
        in_specs=[V, V, V, V, ANY, V, V],
        out_specs=(V, V, V, ANY),
        scratch_shapes=scratch + sems,
        compiler_params=pltpu.CompilerParams(
            collective_id=0, has_side_effects=True, vmem_limit_bytes=56 * 1024 * 1024),
    )(feats, w_first, w_second, fresh_keys, bank, block_lists, dest_rows.reshape(1, rows))
    results = (grad_first, grad_second, new_bank)
    grad_first, grad_second, new_bank = pl.pallas_call(
        hand_on,
        out_shape=tuple(sds(x.shape, F32) for x in results),
        in_specs=[ANY] * 3,
        out_specs=(ANY,) * 3,
        scratch_shapes=[dma((10,))],
        compiler_params=pltpu.CompilerParams(vmem_limit_bytes=60 * 1024 * 1024),
    )(*results)
    return (loss[:, 0, :R].reshape(rows), grad_first, grad_second, new_bank)


def solution(mesh):
    D = mesh.shape["dp"]
    H = mesh.shape["head"]
    N = mesh.shape["bank"] * H
    return jax.shard_map(
        functools.partial(shards, D, N, H),
        mesh=mesh,
        in_specs=(
            P("dp", None),
            P(None, ("bank", "head")),
            P(("bank", "head"), None),
            P("dp", None),
            P(("bank", "head"), None),
            P("dp", None),
            P("dp"),
        ),
        out_specs=(
            P("dp"),
            P("dp", ("bank", "head")),
            P(("bank", "head"), None),
            P(("bank", "head"), None),
        ),
        check_vma=False,
    )
```

```python
import functools
import math

import jax
import jax.numpy as jnp
from jax import lax
from jax.experimental import pallas as pl
from jax.experimental.pallas import tpu as pltpu
from jax.sharding import PartitionSpec as P

BLOCK = 512
EPS = 1e-6
SCALE = 5.0
LOG2E = 1.4426950408889634
LN2 = 0.6931471805599453
LOWEST = -1e30
MESH = pl.DeviceIdType.MESH
F32 = jnp.float32
BF16 = jnp.bfloat16


def nt(a, b, **kw):
    return lax.dot_general(a, b, (((1,), (1,)), ((), ())), preferred_element_type=F32, **kw)


def tn(a, b):
    return lax.dot_general(a, b, (((0,), (0,)), ((), ())), preferred_element_type=F32)


def body(
    D, N, H,
    feats, w1, w2, fresh, bank, lists, dest,
    loss_out, gf_out, gs_out, bank_out,
    hid, zp, zr, zs, zfull, kcat, qcat, sbuf, acc, ml, ar, mr, st, gz, gfull, lt, lr,
    gfs, gfr, gfl, gsp, gsr, gst, gsf, ks, kr, kd, kdr,
    s_z, r_z, s_q, r_q, s_a, r_a, s_m, r_m, s_g, r_g, s_l, r_l,
    s_f, r_f, s_s, r_s, s_t, r_t, s_k, r_k, s_d, r_d, s_fl, r_fl, bvm, s_b, s_o, k3, zh,
):
    d = lax.axis_index("dp")
    bk = lax.axis_index("bank")
    hd = lax.axis_index("head")
    me = bk * H + hd
    rows = zp.shape[0]
    R = rows // N
    nblk = kcat.shape[0]

    def plane(k):
        p = lax.rem(me + k, N)
        return p, {"bank": lax.div(p, H), "head": lax.rem(p, H)}

    def line(j):
        p = lax.rem(d + j, D)
        return p, {"dp": p}

    def chunk(p, size):
        return pl.ds(pl.multiple_of(p * size, size), size)

    def send(src, dst, ss, rs, dev):
        c = pltpu.make_async_remote_copy(
            src_ref=src, dst_ref=dst, send_sem=ss, recv_sem=rs,
            device_id=dev, device_id_type=MESH)
        c.start()
        return c

    def load(b):
        at = pl.ds(pl.multiple_of(b * BLOCK, BLOCK), BLOCK)
        return pltpu.make_async_copy(bank.at[at], bvm.at[at], s_b.at[b])

    for b in range(nblk):
        load(b).start()
    C = N // H
    sibling = {"head": 1 - hd}

    def gather_rows(mine, full, ss, rs):
        at = full.at[chunk(me, R)]
        away = []
        for i in range(1, C):
            dev = {"bank": lax.rem(bk + i, C)}
            away.append(send(mine, at, ss.at[i], rs.at[i], dev))
        near = [send(mine, at, ss.at[C], rs.at[C], sibling)]
        for i in range(1, C):
            away[i - 1].wait_recv()
            came = full.at[chunk(lax.rem(bk + C - i, C) * H + hd, R)]
            near.append(send(came, came, ss.at[C + i], rs.at[C + i], sibling))
        for c in near:
            c.wait_recv()
        return away + near

    barrier = pltpu.get_barrier_semaphore()
    for k in range(1, N):
        pl.semaphore_signal(barrier, inc=1, device_id=plane(k)[1], device_id_type=MESH)
    for j in range(1, D):
        pl.semaphore_signal(barrier, inc=1, device_id=line(j)[1], device_id_type=MESH)

    h = jnp.maximum(jnp.dot(feats[...], w1[...], preferred_element_type=F32), 0.0).astype(BF16)
    hid[...] = h
    zp[...] = jnp.dot(h, w2[...], preferred_element_type=F32)
    pl.semaphore_wait(barrier, N - 1 + D - 1)

    pending = []
    z_copies = []
    turns = [*range(1, C), 0]
    for i in turns:
        part = zp.at[chunk(lax.rem(bk + i, C) * H + 1 - hd, R)]
        z_copies.append(send(part, zr.at[i], s_z.at[i], r_z.at[i], sibling))
    z_away = []
    for i in turns:
        z_copies[turns.index(i)].wait_recv()
        c = lax.rem(bk + i, C)
        zh[i] = zp[chunk(c * H + hd, R), :] + zr[i]
        if i:
            z_away.append(send(zh.at[i], zr.at[C + i], s_z.at[C + i], r_z.at[C + i], {"bank": c}))

    f = fresh[...]
    unit = f / jnp.sqrt(jnp.sum(f * f, axis=1, keepdims=True) + EPS)
    local = jnp.broadcast_to(dest[...].astype(F32), (8, rows)) - (me * bank.shape[0]).astype(F32)
    inside = (local >= 0.0) & (local < float(bank.shape[0]))
    one = jnp.where(inside, 1.0, 0.0)
    upper = lax.broadcasted_iota(jnp.int32, (rows, rows), 0) <= lax.broadcasted_iota(
        jnp.int32, (rows, rows), 1)
    place = jnp.dot(one.astype(BF16), jnp.where(upper, 1.0, 0.0).astype(BF16),
                    preferred_element_type=F32) * one
    want = lax.broadcasted_iota(jnp.int32, (128, rows), 0).astype(F32) + 1.0
    pick = jnp.where(want == jnp.broadcast_to(place[0:1, :], (128, rows)), 1.0, 0.0)
    ks[...] = jnp.dot(pick[0:R], unit, precision=lax.Precision.HIGHEST, preferred_element_type=F32)
    spots = nt(jnp.where(inside, local, 0.0), pick, precision=lax.Precision.HIGHEST)
    kd[...] = jnp.floor(spots + 0.5)
    for j in range(1, D):
        dev = line(j)[1]
        pending.append(send(ks, kr.at[j], s_k.at[j], r_k.at[j], dev))
        pending.append(send(kd, kdr.at[j], s_d.at[j], r_d.at[j], dev))
    kr[0] = ks[...]
    kdr[0] = kd[...]

    def split(b, carry):
        load(b).wait()
        x = bvm[pl.ds(pl.multiple_of(b * BLOCK, BLOCK), BLOCK), :]
        hi = x.astype(BF16)
        lo = (x - hi.astype(F32)).astype(BF16)
        kcat[b, :, 0:256] = hi
        kcat[b, :, 256:512] = lo
        kcat[b, :, 512:768] = hi
        return carry

    lax.fori_loop(0, nblk, split, 0)

    total_z = zh[0]
    for i in range(1, C):
        z_away[i - 1].wait_recv()
        total_z = total_z + zr[C + i]
    zs[...] = total_z
    zfull[chunk(me, R), :] = total_z
    q_copies = gather_rows(zs, zfull, s_q, r_q)
    z = zfull[...]
    q = z / jnp.sqrt(jnp.sum(z * z, axis=1, keepdims=True) + EPS) * (SCALE * LOG2E)
    qh = q.astype(BF16)
    qcat[:, 0:256] = qh
    qcat[:, 256:512] = qh
    qcat[:, 512:768] = (q - qh.astype(F32)).astype(BF16)

    def scores(b, best):
        hit = jnp.max(jnp.where(lists[...] == me * nblk + b, 0.0, LOWEST), axis=1, keepdims=True)
        s = nt(qcat[...], kcat[b]) + hit
        sbuf[b] = s
        for t in range(BLOCK // 128):
            best = jnp.maximum(best, s[:, t * 128:(t + 1) * 128])
        return best

    best = lax.fori_loop(0, nblk, scores, jnp.full((rows, 128), LOWEST, F32))
    best = jnp.max(best, axis=1, keepdims=True)
    acc[...] = jnp.zeros_like(acc)

    def mix(b, total):
        w = jnp.exp2(sbuf[b] - best)
        for t in range(BLOCK // 128):
            total = total + w[:, t * 128:(t + 1) * 128]
        both = jnp.dot(w.astype(BF16), kcat[b, :, 0:512], preferred_element_type=F32)
        acc[...] += both[:, 0:256] + both[:, 256:512]
        return total

    total = lax.fori_loop(0, nblk, mix, jnp.zeros((rows, 128), F32))
    total = jnp.sum(total, axis=1, keepdims=True)
    lane = lax.broadcasted_iota(jnp.int32, (rows, 128), 1)
    stat = jnp.where(lane == 0, best, total).T
    for c in range(rows // 128):
        ml[c] = stat[0:8, c * 128:(c + 1) * 128]

    a_copies = []
    per = 128 // R
    for k in range(1, N):
        p, dev = plane(k)
        a_copies.append(send(ml.at[lax.div(p, per)], mr.at[k], s_m.at[k], r_m.at[k], dev))
        a_copies.append(send(acc.at[chunk(p, R)], ar.at[k], s_a.at[k], r_a.at[k], dev))
    mr[0] = ml[lax.div(me, per)]
    for c in a_copies:
        c.wait_recv()
    tiles = mr[...].reshape(N * 8, 128)
    st[...] = jnp.concatenate([tiles, jnp.zeros((128 - N * 8, 128), F32)], axis=0).T
    stats = st[chunk(lax.rem(me, per), R), :]

    zc = zfull[chunk(me, R), :]
    norm = jnp.sqrt(jnp.sum(zc * zc, axis=1, keepdims=True) + EPS)
    qc = zc / norm
    fc = fresh[chunk(me, R), :]
    uc = fc / jnp.sqrt(jnp.sum(fc * fc, axis=1, keepdims=True) + EPS)
    pos = jnp.sum(qc * uc, axis=1, keepdims=True) * (SCALE * LOG2E)
    top = pos
    for k in range(N):
        top = jnp.maximum(top, stats[:, k * 8:k * 8 + 1])
    pw = jnp.exp2(pos - top)
    den = pw
    mixed = jnp.zeros((R, acc.shape[1]), F32)
    for k in range(N):
        wk = jnp.exp2(stats[:, k * 8:k * 8 + 1] - top)
        den = den + wk * stats[:, k * 8 + 1:k * 8 + 2]
        mixed = mixed + wk * (acc[chunk(me, R), :] if k == 0 else ar[k])
    losses = (top - pos) * LN2 + jnp.log(den)
    gq = (mixed / den + (pw / den - 1.0) * uc) * SCALE
    inner = jnp.sum(qc * gq, axis=1, keepdims=True)
    g = ((gq - qc * inner) / norm).astype(BF16).astype(F32)
    gz[...] = g
    gfull[chunk(me, R), :] = g
    wide = jnp.concatenate(
        [jnp.broadcast_to(losses, (R, 128)), jnp.zeros((128 - R, 128), F32)], axis=0)
    lt[...] = wide.T[0:8, :]
    lr[me] = lt[...]
    for k in range(1, N):
        pending.append(send(lt, lr.at[me], s_l.at[k], r_l.at[k], plane(k)[1]))
    g_copies = gather_rows(gz, gfull, s_g, r_g)

    gb = gfull[...].astype(BF16)
    gsp[...] = tn(hid[...], gb)
    S = gsp.shape[0] // D
    s_copies = []
    for j in range(1, D):
        p, dev = line(j)
        s_copies.append(send(gsp.at[chunk(p, S)], gsr.at[j], s_s.at[j], r_s.at[j], dev))
    gp = nt(gb, w2[...])
    gp = jnp.where(hid[...] > 0, gp, 0.0).astype(BF16)
    F = gf_out.shape[0]
    if F % 128:
        for t in range(feats.shape[1] // 256):
            gfs[t * 256:(t + 1) * 256, :] = tn(feats[:, t * 256:(t + 1) * 256], gp)

    def hop(p, nxt, got, ss, rs):
        return pltpu.make_async_remote_copy(
            src_ref=gfs.at[chunk(p, F)], dst_ref=got.at[p], send_sem=ss.at[p],
            recv_sem=rs.at[p], device_id={"dp": nxt}, device_id_type=MESH)

    def step(p, first, nxt, got, ss, rs):
        if F % 128 == 0:
            gfs[chunk(p, F), :] = tn(feats[:, chunk(p, F)], gp)
        move = hop(p, nxt, got, ss, rs)

        @pl.when(jnp.logical_not(first))
        def _():
            move.wait_recv()
            gfs[chunk(p, F), :] += got[p]

        move.start()

    up = lax.min(d + 1, D - 1)
    down = lax.max(d - 1, 0)

    def both_ways(t, act):
        @pl.when(d <= t)
        def _():
            act(D - 1 - t + d, d == 0, up, gfr, s_f, r_f)

        @pl.when(d >= D - 1 - t)
        def _():
            act(t - (D - 1 - d), d == D - 1, down, gfl, s_fl, r_fl)

    t_copies = []
    for t in range(D - 1):
        both_ways(t, step)
        if t == 0:
            total_s = gsp[chunk(d, S), :]
            for j in range(1, D):
                s_copies[j - 1].wait_recv()
                total_s = total_s + gsr[j]
            gst[...] = total_s
            gsf[chunk(d, S), :] = total_s
            for j in range(1, D):
                dev = line(j)[1]
                t_copies.append(send(gst, gsf.at[chunk(d, S)], s_t.at[j], r_t.at[j], dev))
    if F % 128 == 0:
        gf_out[...] = tn(feats[:, chunk(d, F)], gp)
    else:
        gf_out[...] = gfs[chunk(d, F), :]

    for c in pending:
        c.wait_recv()
    spot = jnp.concatenate([kdr[j][0:1, 0:R] for j in range(D)], axis=1)
    k = kr[...].reshape(D * R, kr.shape[2])
    k_hi = k.astype(BF16)
    k = k - k_hi.astype(F32)
    k_mid = k.astype(BF16)
    k3[:, 0:256] = k_hi
    k3[:, 256:512] = k_mid
    k3[:, 512:768] = (k - k_mid.astype(F32)).astype(BF16)

    def store(b):
        at = pl.ds(pl.multiple_of(b * BLOCK, BLOCK), BLOCK)
        return pltpu.make_async_copy(bvm.at[at], bank_out.at[at], s_o.at[b])

    def place_block(b, carry):
        row = (lax.broadcasted_iota(jnp.int32, (BLOCK, D * R), 0) + b * BLOCK).astype(F32)
        one_hot = jnp.where(row == spot, 1.0, 0.0)
        new = jnp.dot(one_hot.astype(BF16), k3[...], preferred_element_type=F32)
        new = new[:, 0:256] + new[:, 256:512] + new[:, 512:768]
        hit = jnp.max(one_hot, axis=1, keepdims=True) > 0.0
        at = pl.ds(pl.multiple_of(b * BLOCK, BLOCK), BLOCK)
        bvm[at, :] = jnp.where(hit, new, bvm[at, :])
        store(b).start()
        return carry

    lax.fori_loop(0, nblk, place_block, 0)
    loss_out[...] = lr[...]
    for c in t_copies:
        c.wait_recv()
    gs_out[...] = gsf[...]

    @pl.when(d > 0)
    def _():
        hop(d, up, gfr, s_f, r_f).wait_recv()
        gf_out[...] += gfr[d]

    @pl.when(d < D - 1)
    def _():
        hop(d, down, gfl, s_fl, r_fl).wait_recv()
        gf_out[...] += gfl[d]

    for b in range(nblk):
        store(b).wait()
    for t in range(D - 1):
        both_ways(t, lambda p, first, nxt, got, ss, rs: hop(p, nxt, got, ss, rs).wait_send())
    for c in z_copies + z_away + q_copies + a_copies + g_copies + s_copies + t_copies + pending:
        c.wait_send()


def hand_on(gf, gs, bank, gf_out, gs_out, bank_out, gf_buf, gs_buf, bank_buf, got, put):
    size = bank.shape[0] // 8
    parts = [(gf, gf_buf, gf_out), (gs, gs_buf, gs_out)]
    for i in range(8):
        at = pl.ds(i * size, size)
        parts.append((bank.at[at], bank_buf.at[at], bank_out.at[at]))
    reads = [pltpu.make_async_copy(p[0], p[1], got.at[i]) for i, p in enumerate(parts)]
    writes = [pltpu.make_async_copy(p[1], p[2], put.at[i]) for i, p in enumerate(parts)]
    for c in reads:
        c.start()
    for r, w in zip(reads, writes):
        r.wait()
        w.start()
    for c in writes:
        c.wait()


def shards(D, N, H, feats, w_first, w_second, fresh_keys, bank, block_lists, dest_rows):
    rows, din = feats.shape
    hcols = w_first.shape[1]
    E = w_second.shape[1]
    nblk = bank.shape[0] // BLOCK
    R = rows // N
    F = din // D
    S = hcols // D
    V = pl.BlockSpec(memory_space=pltpu.VMEM)
    ANY = pl.BlockSpec(memory_space=pl.ANY)
    sds = jax.ShapeDtypeStruct
    vm = pltpu.VMEM
    scratch = [
        vm((rows, hcols), BF16), vm((rows, E), F32), vm((N, R, E), F32), vm((R, E), F32),
        vm((rows, E), F32), vm((nblk, BLOCK, 3 * E), BF16), vm((rows, 3 * E), BF16),
        vm((nblk, rows, BLOCK), F32), vm((rows, E), F32), vm((rows // 128, 8, 128), F32),
        vm((N, R, E), F32), vm((N, 8, 128), F32), vm((128, 128), F32), vm((R, E), F32),
        vm((rows, E), F32), vm((8, 128), F32), vm((N, 8, 128), F32),
        vm((din, hcols), F32), vm((D, F, hcols), F32), vm((D, F, hcols), F32), vm((hcols, E), F32), vm((D, S, E), F32),
        vm((S, E), F32), vm((hcols, E), F32), vm((R, E), F32), vm((D, R, E), F32),
        vm((8, 128), F32), vm((D, 8, 128), F32),
    ]
    dma = pltpu.SemaphoreType.DMA
    sems = [dma((N,))] * 12 + [dma((D,))] * 12 + [vm(bank.shape, F32), dma((nblk,)), dma((nblk,)), vm((D * R, 3 * E), BF16), vm((N // H, R, E), F32)]
    loss, grad_first, grad_second, new_bank = pl.pallas_call(
        functools.partial(body, D, N, H),
        out_shape=(
            sds((N, 8, 128), F32), sds((F, hcols), F32), sds((hcols, E), F32),
            sds(bank.shape, F32),
        ),
        in_specs=[V, V, V, V, ANY, V, V],
        out_specs=(V, V, V, ANY),
        scratch_shapes=scratch + sems,
        compiler_params=pltpu.CompilerParams(
            collective_id=0, has_side_effects=True, vmem_limit_bytes=56 * 1024 * 1024),
    )(feats, w_first, w_second, fresh_keys, bank, block_lists, dest_rows.reshape(1, rows))
    results = (grad_first, grad_second, new_bank)
    grad_first, grad_second, new_bank = pl.pallas_call(
        hand_on,
        out_shape=tuple(sds(x.shape, F32) for x in results),
        in_specs=[ANY] * 3,
        out_specs=(ANY,) * 3,
        scratch_shapes=[vm(x.shape, F32) for x in results] + [dma((10,)), dma((10,))],
        compiler_params=pltpu.CompilerParams(vmem_limit_bytes=60 * 1024 * 1024),
    )(*results)
    return (loss[:, 0, :R].reshape(rows), grad_first, grad_second, new_bank)


def solution(mesh):
    D = mesh.shape["dp"]
    H = mesh.shape["head"]
    N = mesh.shape["bank"] * H
    return jax.shard_map(
        functools.partial(shards, D, N, H),
        mesh=mesh,
        in_specs=(
            P("dp", None),
            P(None, ("bank", "head")),
            P(("bank", "head"), None),
            P("dp", None),
            P(("bank", "head"), None),
            P("dp", None),
            P("dp"),
        ),
        out_specs=(
            P("dp"),
            P("dp", ("bank", "head")),
            P(("bank", "head"), None),
            P(("bank", "head"), None),
        ),
        check_vma=False,
    )
```
